32 devices in a mesh: dp: 8 (over z, x), mp: 4 (over y, core).
Axes of the slice: x: 2, y: 2, z: 4, core: 2. Of those that a mesh axis runs over, the one named last changes fastest.
Arguments:
- tokens: bfloat16 [16384, 2048], P('dp'), may hold values from -0.75 to 0.75
- out_grad: bfloat16 [16384, 2048], P('dp'), may hold values from -3 to 3
- down_rows: bfloat16 [2048, 2048], P(('dp', 'mp')), may hold values from -1 to 1
- up_rows: bfloat16 [2048, 2048], P(('dp', 'mp')), may hold values from -1 to 1
- requests: int32 [32, 32, 2], P(('dp', 'mp')), may hold values from 0 to 64, as said below
- places: int32 [8, 16384, 16], P('mp', 'dp'), may hold values from 0 to 63, as said below
- gate_weights: float32 [8, 16384, 16], P('mp', 'dp'), may hold values from 0.05 to 0.5
Outputs:
- input_grad: bfloat16 [16384, 2048], P(('dp', 'mp'))
- down_grad: float32 [2048, 2048], P(('dp', 'mp'))
- up_grad: float32 [2048, 2048], P(('dp', 'mp'))
The draws below stay inside these ranges and needn't reach their ends.
Inputs may be any that keep to these rules, and one draw needn't show every extreme that they name: requests[d, o] lists distinct rows, numbered within owner o's block of 64, that device d uses; the used ones come first and the rest of the 2 places hold 64. Every device uses at least one row of every owner, and all 2 places of some owner. The 16 entries of one head and token are distinct places, each of which names an expert in the request list of the device holding that head and token.
All inputs are finite; a program needn't handle non-finite values.
Results may differ from the reference program's by a relative error of at most 0.013.
Values may be sent and summed in bfloat16 or wider, within the bound.
A program may use at most 128 MiB of HBM per device.

```python
import math
import jax
import jax.numpy as jnp
from jax import lax

D = 2048
HEADS = 8
TOPK = 16
TOK_DEV = 2048
HOT_DEV = 64
UCAP = 2
HEADS_DEV = 2
HOT = 2048
SLOTS = 64
TOKENS = 16384
N_MP = 4
DEVICES = 32


def request_lists(key):
    count_key, full_key, order_key = jax.random.split(jax.random.fold_in(key, 101), 3)
    counts = jax.random.randint(count_key, (DEVICES, DEVICES), 1, UCAP + 1)
    full_owner = jax.random.randint(full_key, (DEVICES,), 0, DEVICES)
    owner_index = jnp.arange(DEVICES)[None, :]
    counts = jnp.where(owner_index == full_owner[:, None], UCAP, counts)
    scores = jax.random.randint(order_key, (DEVICES, DEVICES, HOT_DEV), 0, 1 << 20) * HOT_DEV + jnp.arange(HOT_DEV)[None, None, :]
    chosen = jnp.argsort(scores, axis=-1)[:, :, :UCAP]
    position = jnp.arange(UCAP)[None, None, :]
    return jnp.where(position < counts[:, :, None], chosen, HOT_DEV).astype(jnp.int32)


def draw_requests(key, part):
    return request_lists(key)


def draw_places(key, part):
    lists = request_lists(key).reshape(DEVICES, SLOTS)
    live = lists < HOT_DEV
    popular_key, noise_key = jax.random.split(jax.random.fold_in(key, 202))
    popular = jax.random.randint(popular_key, (DEVICES, SLOTS), 0, 1 << 10)
    slot_index = jnp.arange(SLOTS)[None, :]

    def one_head(head):
        noise = jax.random.randint(jax.random.fold_in(noise_key, head), (TOKENS, SLOTS), 0, 1 << 10)
        device = jnp.arange(TOKENS) // TOK_DEV * N_MP + head // HEADS_DEV
        score = (popular[device] + noise) * SLOTS + slot_index
        score = jnp.where(live[device], score, -1 - slot_index)
        return lax.top_k(score, TOPK)[1].astype(jnp.int32)
    return lax.map(one_head, jnp.arange(HEADS))


def level_of(stream_key, dims, cuts, smallest, high):
    gain = 1.0
    for axis_at, shards_of in cuts:
        steps = jax.random.uniform(jax.random.fold_in(jax.random.fold_in(stream_key, 6), axis_at), (shards_of,), jnp.float32, smallest / len(cuts), high / len(cuts))
        gain = gain * jnp.repeat(jnp.exp(steps), dims[axis_at] // shards_of).reshape((-1,) + (1,) * (len(dims) - 1 - axis_at))
    return gain


def gaussian(stream_key, extent, spread, reach, cuts=(), kind=jnp.bfloat16):
    values = jax.random.normal(stream_key, extent, jnp.float32) * spread
    if len(cuts) > 0:
        values = level_of(stream_key, extent, cuts, -0.22, 0.18) * values
    return jnp.clip(values, min=-reach, max=reach).astype(kind)


def setup_inputs(seed: int = 0) -> dict:
    seeds = jax.random.split(jax.random.key(seed), 8)
    return {
        "tokens": gaussian(seeds[0], (TOKENS, D), 0.125, 0.75, ((0, 8),)),
        "out_grad": gaussian(seeds[1], (TOKENS, D), 0.5, 3.0, ((0, 8),)),
        "down_rows": gaussian(seeds[2], (HOT, D), (D // 64) ** -0.5, 1.0, ((0, 32),)),
        "up_rows": gaussian(seeds[3], (HOT, D), (D // 48) ** -0.5, 1.0, ((0, 32),)),
        "requests": draw_requests(jax.random.fold_in(seeds[7], 71), 0),
        "places": draw_places(jax.random.fold_in(seeds[7], 71), 0),
        "gate_weights": jnp.clip(jnp.exp(math.log(0.5) - 2.3025851 * jax.random.uniform(seeds[6], (HEADS, TOKENS, TOPK), jnp.float32) ** level_of(seeds[6], (HEADS, TOKENS, TOPK), ((0, 4), (1, 8)), -0.2, 0.2)), 0.05, 0.5),
    }


SQRT_HALF = 0.7071067811865476
INV_ROOT_TAU = 0.3989422804014327


def gelu_parts(pre):
    normal_cdf = 0.5 * (1.0 + lax.erf(pre * SQRT_HALF))
    density = INV_ROOT_TAU * jnp.exp(-0.5 * pre * pre)
    return pre * normal_cdf, normal_cdf + pre * density


def local_terms(block_tokens, block_grad, fetched_down, fetched_up, block_places, block_gates):
    token_count = block_tokens.shape[0]
    place_count = fetched_down.shape[0]
    chosen = jnp.transpose(block_places, (1, 0, 2)).reshape(token_count, -1)
    weights_in = jnp.transpose(block_gates, (1, 0, 2)).reshape(token_count, -1)
    columns = jnp.arange(place_count, dtype=jnp.int32)
    weight = jnp.sum(jnp.where(chosen[:, :, None] == columns[None, None, :], weights_in[:, :, None], jnp.zeros((), weights_in.dtype)), axis=1)
    pre = lax.dot_general(block_tokens, fetched_down, (((1,), (1,)), ((), ())), preferred_element_type=jnp.float32)
    back = lax.dot_general(block_grad, fetched_up, (((1,), (1,)), ((), ())), preferred_element_type=jnp.float32)
    active, slope = gelu_parts(pre)
    coef = (weight * slope * back).astype(jnp.bfloat16)
    gated = (weight * active).astype(jnp.bfloat16)
    part_down = lax.dot_general(coef, block_tokens, (((0,), (0,)), ((), ())), preferred_element_type=jnp.float32)
    part_up = lax.dot_general(gated, block_grad, (((0,), (0,)), ((), ())), preferred_element_type=jnp.float32)
    return coef, part_down, part_up


def reference(tokens, out_grad, down_rows, up_rows, requests, places, gate_weights):
    owner_base = jnp.arange(DEVICES, dtype=jnp.int32)[:, None] * HOT_DEV

    def visit(carry, device):
        down_acc, up_acc, input_acc = carry
        row_block = device // N_MP
        col_block = device % N_MP
        asked = lax.dynamic_index_in_dim(requests, device, 0, keepdims=False)
        live = (asked < HOT_DEV).reshape(-1)
        experts = (owner_base + jnp.minimum(asked, HOT_DEV - 1)).reshape(-1).astype(jnp.int32)
        fetched_down = jnp.where(live[:, None], down_rows[experts], jnp.zeros((), down_rows.dtype))
        fetched_up = jnp.where(live[:, None], up_rows[experts], jnp.zeros((), up_rows.dtype))
        token_start = (row_block * TOK_DEV).astype(jnp.int32)
        head_start = (col_block * HEADS_DEV).astype(jnp.int32)
        zero_index = jnp.zeros((), jnp.int32)
        block_tokens = lax.dynamic_slice_in_dim(tokens, token_start, TOK_DEV, 0)
        block_grad = lax.dynamic_slice_in_dim(out_grad, token_start, TOK_DEV, 0)
        block_places = lax.dynamic_slice(places, (head_start, token_start, zero_index), (HEADS_DEV, TOK_DEV, TOPK))
        block_gates = lax.dynamic_slice(gate_weights, (head_start, token_start, zero_index), (HEADS_DEV, TOK_DEV, TOPK))
        coef, part_down, part_up = local_terms(block_tokens, block_grad, fetched_down, fetched_up, block_places, block_gates)
        partial_value = jnp.dot(coef, fetched_down, preferred_element_type=jnp.float32).astype(jnp.bfloat16)
        targets = jnp.where(live, experts, HOT).astype(jnp.int32)
        down_acc = down_acc.at[targets].add(part_down, mode="drop")
        up_acc = up_acc.at[targets].add(part_up, mode="drop")
        previous = lax.dynamic_slice_in_dim(input_acc, token_start, TOK_DEV, 0)
        input_acc = lax.dynamic_update_slice_in_dim(input_acc, previous + partial_value.astype(jnp.float32), token_start, 0)
        return (down_acc, up_acc, input_acc), None

    start = (jnp.zeros((HOT, D), jnp.float32), jnp.zeros((HOT, D), jnp.float32), jnp.zeros((TOKENS, D), jnp.float32))
    final, _ = lax.scan(visit, start, jnp.arange(DEVICES, dtype=jnp.int32))
    down_grad, up_grad, input_acc = final
    return input_acc.astype(jnp.bfloat16), down_grad, up_grad
```

```python
import jax
import jax.numpy as jnp
from jax import lax
from jax.sharding import PartitionSpec as P

SQRT_HALF = 0.7071067811865476
INV_ROOT_TAU = 0.3989422804014327


def gelu_parts(pre):
    normal_cdf = 0.5 * (1.0 + lax.erf(pre * SQRT_HALF))
    density = INV_ROOT_TAU * jnp.exp(-0.5 * pre * pre)
    return (pre * normal_cdf, normal_cdf + pre * density)


def local_terms(block_tokens, block_grad, fetched_down, fetched_up, block_places, block_gates):
    token_count = block_tokens.shape[0]
    place_count = fetched_down.shape[0]
    chosen = jnp.transpose(block_places, (1, 0, 2)).reshape(token_count, -1)
    weights_in = jnp.transpose(block_gates, (1, 0, 2)).reshape(token_count, -1)
    columns = jnp.arange(place_count, dtype=jnp.int32)
    weight = jnp.sum(
        jnp.where(
            chosen[:, :, None] == columns[None, None, :],
            weights_in[:, :, None],
            jnp.zeros((), weights_in.dtype),
        ),
        axis=1,
    )
    pre = lax.dot_general(
        block_tokens, fetched_down, (((1,), (1,)), ((), ())), preferred_element_type=jnp.float32
    )
    back = lax.dot_general(
        block_grad, fetched_up, (((1,), (1,)), ((), ())), preferred_element_type=jnp.float32
    )
    active, slope = gelu_parts(pre)
    coef = (weight * slope * back).astype(jnp.bfloat16)
    gated = (weight * active).astype(jnp.bfloat16)
    part_down = lax.dot_general(
        coef, block_tokens, (((0,), (0,)), ((), ())), preferred_element_type=jnp.float32
    )
    part_up = lax.dot_general(
        gated, block_grad, (((0,), (0,)), ((), ())), preferred_element_type=jnp.float32
    )
    return (coef, part_down, part_up)


def shards(tokens, out_grad, down_rows, up_rows, requests, places, gate_weights):
    n_data = lax.axis_size("dp")
    n_model = lax.axis_size("mp")
    devices = n_data * n_model
    row_count = down_rows.shape[0]
    width = tokens.shape[1]
    wanted = requests[0]
    capacity = wanted.shape[1]
    asked = lax.all_to_all(wanted, ("dp", "mp"), split_axis=0, concat_axis=0, tiled=True)
    live = (wanted < row_count).reshape(-1)
    table = jnp.concatenate([down_rows, up_rows], axis=1)
    outgoing = jnp.take(table, jnp.minimum(asked, row_count - 1).reshape(-1), axis=0).reshape(
        devices, capacity, 2 * width
    )
    arrived = lax.all_to_all(outgoing, ("dp", "mp"), split_axis=0, concat_axis=0, tiled=True)
    arrived = arrived.reshape(devices * capacity, 2 * width)
    arrived = jnp.where(live[:, None], arrived, jnp.zeros((), arrived.dtype))
    fetched_down = arrived[:, :width]
    fetched_up = arrived[:, width:]
    coef, part_down, part_up = local_terms(
        tokens, out_grad, fetched_down, fetched_up, places, gate_weights
    )
    token_count = tokens.shape[0] // n_model
    group_down = lax.all_gather(fetched_down, "mp", axis=0, tiled=True)
    mine = lax.all_to_all(
        coef.reshape(n_model, token_count, -1), "mp", split_axis=0, concat_axis=0, tiled=True
    )
    mine = jnp.transpose(mine, (1, 0, 2)).reshape(token_count, -1)
    pushed = jnp.concatenate([part_down, part_up], axis=1).reshape(devices, capacity, 2 * width)
    returned = lax.all_to_all(
        pushed.astype(jnp.bfloat16), ("dp", "mp"), split_axis=0, concat_axis=0, tiled=True
    ).astype(pushed.dtype)
    returned = returned.reshape(devices * capacity, 2 * width)
    selector = (asked.reshape(1, -1) == jnp.arange(row_count, dtype=jnp.int32)[:, None]).astype(
        jnp.float32
    )
    summed = jnp.dot(
        selector, returned, precision=lax.Precision.HIGHEST, preferred_element_type=jnp.float32
    )
    down_grad = summed[:, :width]
    up_grad = summed[:, width:]
    input_grad = jnp.dot(
        mine, group_down, preferred_element_type=jnp.float32
    ).astype(jnp.bfloat16)
    return (input_grad, down_grad, up_grad)


def solution(mesh):
    in_specs = (
        P("dp", None),
        P("dp", None),
        P(("dp", "mp"), None),
        P(("dp", "mp"), None),
        P(("dp", "mp"), None, None),
        P("mp", "dp", None),
        P("mp", "dp", None),
    )
    out_specs = (P(("dp", "mp"), None), P(("dp", "mp"), None), P(("dp", "mp"), None))
    return jax.shard_map(shards, mesh=mesh, in_specs=in_specs, out_specs=out_specs, check_vma=False)
```

```python
import functools

import jax
import jax.numpy as jnp
from jax import lax
from jax.experimental import pallas as pl
from jax.experimental.pallas import tpu as pltpu
from jax.sharding import PartitionSpec as P

SQRT_HALF = 0.7071067811865476
INV_ROOT_TAU = 0.3989422804014327
F32 = jnp.float32
BF16 = jnp.bfloat16
GROUP = 8
MESH = pl.DeviceIdType.MESH


def gelu_parts(pre):
    normal_cdf = 0.5 * (1.0 + lax.erf(pre * SQRT_HALF))
    density = INV_ROOT_TAU * jnp.exp(-0.5 * pre * pre)
    return (pre * normal_cdf, normal_cdf + pre * density)


def iota(shape, dim):
    return lax.broadcasted_iota(jnp.int32, shape, dim)


def ones_where(mask):
    return jnp.where(mask, jnp.float32(1), jnp.float32(0)).astype(BF16)


def dot(a, b, dims=((1,), (0,))):
    return lax.dot_general(a, b, (dims, ((), ())), preferred_element_type=F32)


def kernel(
    n, n_model, tokens, grads, down_rows, up_rows, wanted, places, gates,
    input_grad, down_grad, up_grad,
    tok, grd, asked, table, sel_t, msg_out, msg_in, ret_out, ret_in,
    f_down, f_up, weight, coef_out, coef_in, coef_t, part_down, part_up,
    tok_sem, grd_sem, ask_send, ask_recv, row_send, row_recv, ret_send, ret_recv,
    down_send, down_recv, coef_send, coef_recv, self_sem,
):
    data_at = lax.axis_index("dp")
    model_at = lax.axis_index("mp")
    me = data_at * n_model + model_at
    rows, width = down_rows.shape
    capacity = ret_in.shape[0] // n // 8
    chunk = msg_out.shape[1]
    per_row = 2 * width // chunk
    message = capacity * per_row
    half = width // chunk
    slots = n * capacity
    n_tok = tok.shape[0]
    block = n_tok // n_model
    big = GROUP * message
    groups = n // GROUP

    def tok_copy(j):
        at = pl.ds(j * block, block)
        return pltpu.make_async_copy(tokens.at[at, :], tok.at[at, :], tok_sem.at[j])

    def grd_copy(j):
        at = pl.ds(j * block, block)
        return pltpu.make_async_copy(grads.at[at, :], grd.at[at, :], grd_sem.at[j])

    for j in range(n_model):
        tok_copy(j).start()
        grd_copy(j).start()

    def peer_of(k):
        peer = lax.rem(me + k, n)
        return peer, (lax.div(peer, n_model), lax.rem(peer, n_model))

    barrier = pltpu.get_barrier_semaphore()

    def greet(k, c):
        pl.semaphore_signal(barrier, inc=1, device_id=peer_of(k)[1], device_id_type=MESH)
        return c

    lax.fori_loop(1, n, greet, 0)

    for c in range(per_row):
        source = down_rows if c < half else up_rows
        at = (c % half) * chunk
        table[c * rows:(c + 1) * rows, :] = source[:, at:at + chunk]

    pl.semaphore_wait(barrier, n - 1)

    def ask_copy(k):
        peer, where = peer_of(k)
        return pltpu.make_async_remote_copy(
            src_ref=wanted.at[peer], dst_ref=asked.at[me], send_sem=ask_send.at[peer],
            recv_sem=ask_recv.at[me], device_id=where, device_id_type=MESH)

    def ask_start(k, c):
        ask_copy(k).start()
        return c

    lax.fori_loop(1, n, ask_start, 0)
    own_ask = pltpu.make_async_copy(wanted.at[me], asked.at[me], self_sem.at[0])
    own_ask.start()

    lanes = 256
    pairs = places.shape[0]

    def weigh(i, c):
        at = pl.ds(pl.multiple_of(i * lanes, lanes), lanes)
        for s0 in range(0, slots, 64):
            place = iota((64, lanes), 0) + s0
            total = jnp.zeros((64, lanes), F32)
            for p in range(pairs):
                total += jnp.where(places[p:p + 1, at] == place, gates[p:p + 1, at], jnp.float32(0))
            weight[s0:s0 + 64, at] = total
        return c

    lax.fori_loop(0, n_tok // lanes, weigh, 0)

    own_ask.wait()

    def ask_wait(k, c):
        src = lax.rem(me + n - k, n)
        pltpu.make_async_copy(asked.at[src], asked.at[src], ask_recv.at[src]).wait()
        return c

    lax.fori_loop(1, n, ask_wait, 0)

    def select(g):
        ask = asked[g * GROUP:(g + 1) * GROUP, 0, :].astype(F32)
        first = jnp.broadcast_to(ask[:, 0:1], (GROUP, 128))
        second = jnp.broadcast_to(ask[:, 64:65], (GROUP, 128))
        both = jnp.concatenate([first, second], axis=0)
        r = iota((big, capacity * GROUP), 0)
        c = iota((big, capacity * GROUP), 1)
        spread = ones_where(
            (lax.rem(c, GROUP) == lax.div(r, message))
            & (lax.div(c, GROUP) == lax.div(lax.rem(r, message), per_row)))
        wide = dot(spread, both.astype(BF16))
        lane = iota((big, 128), 1)
        value = wide.astype(jnp.int32)
        parts = []
        tiles = per_row * rows // 128
        for t in range(tiles):
            full = lane + t * 128
            hit = (lax.rem(full, rows) == value) & (
                lax.div(full, rows) == lax.rem(iota((big, 128), 0), per_row))
            parts.append(jnp.where(hit, jnp.float32(1), jnp.float32(0)))
        return jnp.concatenate(parts, axis=1)

    def row_copy(peer):
        at = pl.ds(pl.multiple_of(peer * message, message), message)
        mine = pl.ds(pl.multiple_of(me * message, message), message)
        return pltpu.make_async_remote_copy(
            src_ref=msg_out.at[at, :], dst_ref=msg_in.at[mine, :], send_sem=row_send.at[peer],
            recv_sem=row_recv.at[me],
            device_id=(lax.div(peer, n_model), lax.rem(peer, n_model)), device_id_type=MESH)

    mine_at = pl.ds(pl.multiple_of(me * message, message), message)
    own_row = pltpu.make_async_copy(msg_out.at[mine_at, :], msg_in.at[mine_at, :], self_sem.at[1])

    for g in range(groups):
        sel = select(g)
        sel_t[:, g * big:(g + 1) * big] = sel.T.astype(BF16)
        msg_out[g * big:(g + 1) * big, :] = dot(sel.astype(BF16), table[...]).astype(BF16)

    def row_start(k, c):
        row_copy(peer_of(k)[0]).start()
        return c

    lax.fori_loop(1, n, row_start, 0)
    own_row.start()
    own_row.wait()

    def row_wait(k, c):
        src = lax.rem(me + n - k, n)
        at = pl.ds(pl.multiple_of(src * message, message), message)
        pltpu.make_async_copy(msg_in.at[at, :], msg_in.at[at, :], row_recv.at[src]).wait()
        return c

    lax.fori_loop(1, n, row_wait, 0)

    seats = GROUP * capacity
    r = iota((big, big), 0)
    c = iota((big, big), 1)
    unpack = ones_where((lax.div(r, seats) == lax.rem(c, per_row)) & (lax.rem(r, seats) == lax.div(c, per_row)))
    pack = ones_where((lax.div(c, seats) == lax.rem(r, per_row)) & (lax.rem(c, seats) == lax.div(r, per_row)))
    own_down = pl.ds(pl.multiple_of(model_at * slots, slots), slots)
    for g in range(groups):
        laid = dot(unpack, msg_in[g * big:(g + 1) * big, :]).astype(BF16)
        for j in range(half):
            down_piece = laid[j * seats:(j + 1) * seats, :]
            up_piece = laid[(half + j) * seats:(half + j + 1) * seats, :]
            at = pl.ds(pl.multiple_of(model_at * slots + g * seats, seats), seats)
            f_down[at, j * chunk:(j + 1) * chunk] = down_piece
            f_up[g * seats:(g + 1) * seats, j * chunk:(j + 1) * chunk] = up_piece

    def down_copy(k):
        to = lax.rem(model_at + k, n_model)
        return pltpu.make_async_remote_copy(
            src_ref=f_down.at[own_down, :], dst_ref=f_down.at[own_down, :],
            send_sem=down_send.at[k], recv_sem=down_recv.at[k],
            device_id=(data_at, to), device_id_type=MESH)

    for k in range(1, n_model):
        down_copy(k).start()

    def coef_copy(j, k):
        return pltpu.make_async_remote_copy(
            src_ref=coef_out.at[j], dst_ref=coef_in.at[own_down, :],
            send_sem=coef_send.at[k], recv_sem=coef_recv.at[k],
            device_id=(data_at, j), device_id_type=MESH)

    for b in range(n_model):
        tok_copy(b).wait()
        grd_copy(b).wait()
        at = pl.ds(b * block, block)
        x = tok[at, :]
        y = grd[at, :]
        pre = dot(f_down[own_down, :], x, ((1,), (1,)))
        back = dot(f_up[...], y, ((1,), (1,)))
        w = weight[:, b * block:(b + 1) * block]
        active, slope = gelu_parts(pre)
        coef = (w * slope * back).astype(BF16)
        gated = (w * active).astype(BF16)
        coef_out[b] = coef
        if b == 0:
            part_down[...] = dot(coef, x)
            part_up[...] = dot(gated, y)
        else:
            part_down[...] += dot(coef, x)
            part_up[...] += dot(gated, y)

    for g in range(groups):
        pieces = []
        for source in (part_down, part_up):
            for j in range(half):
                pieces.append(source[g * seats:(g + 1) * seats, j * chunk:(j + 1) * chunk].astype(BF16))
        ret_out[g * big:(g + 1) * big, :] = dot(pack, jnp.concatenate(pieces, axis=0)).astype(BF16)

    def ret_copy(peer):
        at = pl.ds(pl.multiple_of(peer * message, message), message)
        return pltpu.make_async_remote_copy(
            src_ref=ret_out.at[at, :], dst_ref=ret_in.at[mine_at, :], send_sem=ret_send.at[peer],
            recv_sem=ret_recv.at[me],
            device_id=(lax.div(peer, n_model), lax.rem(peer, n_model)), device_id_type=MESH)

    for k in range(1, n_model):
        coef_copy(lax.rem(model_at + k, n_model), k).start()

    def ret_start(k, c):
        ret_copy(peer_of(k)[0]).start()
        return c

    lax.fori_loop(1, n, ret_start, 0)
    own_ret = pltpu.make_async_copy(ret_out.at[mine_at, :], ret_in.at[mine_at, :], self_sem.at[2])
    own_ret.start()

    own_coef = pltpu.make_async_copy(coef_out.at[model_at], coef_in.at[own_down, :], self_sem.at[3])
    own_coef.start()
    own_coef.wait()
    for k in range(1, n_model):
        frm = lax.rem(model_at + n_model - k, n_model)
        there = pl.ds(pl.multiple_of(frm * slots, slots), slots)
        pltpu.make_async_copy(coef_in.at[there, :], coef_in.at[there, :], coef_recv.at[k]).wait()
        pltpu.make_async_copy(f_down.at[there, :], f_down.at[there, :], down_recv.at[k]).wait()
    coef_t[...] = coef_in[...].astype(F32).T.astype(BF16)

    def finish(i, c):
        at = pl.ds(pl.multiple_of(i * 512, 512), 512)
        input_grad[:, at] = dot(coef_t[...], f_down[:, at]).astype(BF16)
        return c

    lax.fori_loop(0, width // 512, finish, 0)

    own_ret.wait()

    def ret_wait(k, c):
        src = lax.rem(me + n - k, n)
        at = pl.ds(pl.multiple_of(src * message, message), message)
        pltpu.make_async_copy(ret_in.at[at, :], ret_in.at[at, :], ret_recv.at[src]).wait()
        return c

    lax.fori_loop(1, n, ret_wait, 0)
    for c in range(per_row):
        target = down_grad if c < half else up_grad
        at = (c % half) * chunk
        target[:, at:at + chunk] = dot(sel_t[c * rows:(c + 1) * rows, :], ret_in[...])

    def sent(k, c):
        peer = peer_of(k)[0]
        ask_copy(k).wait_send()
        row_copy(peer).wait_send()
        ret_copy(peer).wait_send()
        return c

    lax.fori_loop(1, n, sent, 0)
    for k in range(1, n_model):
        down_copy(k).wait_send()
        coef_copy(lax.rem(model_at + k, n_model), k).wait_send()


def shards(tokens, out_grad, down_rows, up_rows, requests, places, gate_weights):
    n_model = lax.axis_size("mp")
    n = lax.axis_size("dp") * n_model
    rows, width = down_rows.shape
    n_tok = tokens.shape[0]
    slots = requests.shape[1] * requests.shape[2]
    block = n_tok // n_model
    chunk = 2 * width // 8
    message = requests.shape[2] * 8
    wanted = jnp.repeat(requests[0], 64, axis=1)[:, None, :]
    chosen = jnp.transpose(places, (0, 2, 1)).reshape(-1, n_tok)
    gates = jnp.transpose(gate_weights, (0, 2, 1)).reshape(-1, n_tok)
    vmem = pl.BlockSpec(memory_space=pltpu.VMEM)
    hbm = pl.BlockSpec(memory_space=pl.ANY)
    dma = pltpu.SemaphoreType.DMA
    flops = 10 * n_tok * slots * width
    return pl.pallas_call(
        functools.partial(kernel, n, n_model),
        out_shape=(
            jax.ShapeDtypeStruct((block, width), BF16),
            jax.ShapeDtypeStruct((rows, width), F32),
            jax.ShapeDtypeStruct((rows, width), F32),
        ),
        in_specs=[hbm, hbm, vmem, vmem, vmem, vmem, vmem],
        out_specs=(vmem, vmem, vmem),
        scratch_shapes=[
            pltpu.VMEM((n_tok, width), BF16),
            pltpu.VMEM((n_tok, width), BF16),
            pltpu.VMEM((n, 1, 128), jnp.int32),
            pltpu.VMEM((8 * rows, chunk), BF16),
            pltpu.VMEM((8 * rows, n * message), BF16),
            pltpu.VMEM((n * message, chunk), BF16),
            pltpu.VMEM((n * message, chunk), BF16),
            pltpu.VMEM((n * message, chunk), BF16),
            pltpu.VMEM((n * message, chunk), BF16),
            pltpu.VMEM((n_model * slots, width), BF16),
            pltpu.VMEM((slots, width), BF16),
            pltpu.VMEM((slots, n_tok), F32),
            pltpu.VMEM((n_model, slots, block), BF16),
            pltpu.VMEM((n_model * slots, block), BF16),
            pltpu.VMEM((block, n_model * slots), BF16),
            pltpu.VMEM((slots, width), F32),
            pltpu.VMEM((slots, width), F32),
            dma((n_model,)), dma((n_model,)),
            dma((n,)), dma((n,)), dma((n,)), dma((n,)), dma((n,)), dma((n,)),
            dma((n_model,)), dma((n_model,)), dma((n_model,)), dma((n_model,)),
            dma((4,)),
        ],
        compiler_params=pltpu.CompilerParams(
            collective_id=0, has_side_effects=True, vmem_limit_bytes=60 * 1024 * 1024),
        cost_estimate=pl.CostEstimate(
            flops=flops, bytes_accessed=4 * n_tok * width, transcendentals=2 * n_tok * slots),
    )(tokens, out_grad, down_rows, up_rows, wanted, chosen, gates)


def solution(mesh):
    in_specs = (
        P("dp", None),
        P("dp", None),
        P(("dp", "mp"), None),
        P(("dp", "mp"), None),
        P(("dp", "mp"), None, None),
        P("mp", "dp", None),
        P("mp", "dp", None),
    )
    out_specs = (P(("dp", "mp"), None), P(("dp", "mp"), None), P(("dp", "mp"), None))
    return jax.shard_map(shards, mesh=mesh, in_specs=in_specs, out_specs=out_specs, check_vma=False)
```

```python
import functools
import math

import jax
import jax.numpy as jnp
from jax import lax
from jax.experimental import pallas as pl
from jax.experimental.pallas import tpu as pltpu
from jax.sharding import PartitionSpec as P

SQRT_HALF = 0.7071067811865476
INV_ROOT_TAU = 0.3989422804014327
F32 = jnp.float32
BF16 = jnp.bfloat16
GROUP = 8
PIECES = 8
SPARE = 4 * 1024 * 1024
MESH = pl.DeviceIdType.MESH


def gelu_parts(pre):
    normal_cdf = 0.5 * (1.0 + lax.erf(pre * SQRT_HALF))
    density = INV_ROOT_TAU * jnp.exp(-0.5 * pre * pre)
    return (pre * normal_cdf, normal_cdf + pre * density)


def iota(shape, dim):
    return lax.broadcasted_iota(jnp.int32, shape, dim)


def ones_where(mask):
    return jnp.where(mask, jnp.float32(1), jnp.float32(0)).astype(BF16)


def dot(a, b, dims=((1,), (0,))):
    return lax.dot_general(a, b, (dims, ((), ())), preferred_element_type=F32)


def kernel(
    n, n_model, tokens, grads, down_rows, up_rows, requests, places, gates,
    input_grad, down_grad, up_grad,
    tok, grd, pad, wanted, asked, table, sel, sel_t, msg_out, msg_in, ret_out, ret_in,
    f_down, f_up, weight, gated, coef_out, coef_in, coef_t, part,
    tok_sem, grd_sem, ask_send, ask_recv, row_send, row_recv, ret_send, ret_recv,
    down_send, down_recv, coef_send, coef_recv,
):
    data_at = lax.axis_index("dp")
    model_at = lax.axis_index("mp")
    me = data_at * n_model + model_at
    rows, width = down_rows.shape
    capacity = requests.shape[0]
    per_row = PIECES
    chunk = width // per_row
    message = capacity * per_row
    slots = n * capacity
    n_tok = tok.shape[0]
    block = n_tok // n_model
    big = GROUP * message
    groups = n // GROUP
    lines = n_model // 2

    def tok_copy(j):
        at = pl.ds(j * block, block)
        return pltpu.make_async_copy(tokens.at[at, :], tok.at[at, :], tok_sem.at[j])

    def grd_copy(j):
        at = pl.ds(j * block, block)
        return pltpu.make_async_copy(grads.at[at, :], grd.at[at, :], grd_sem.at[j])

    for j in range(n_model):
        tok_copy(j).start()
    for j in range(n_model):
        grd_copy(j).start()

    def where(peer):
        return (lax.div(peer, n_model), lax.rem(peer, n_model))

    def peer_of(k):
        return lax.rem(me + k, n)

    barrier = pltpu.get_barrier_semaphore()

    def greet(k, c):
        pl.semaphore_signal(barrier, inc=1, device_id=where(peer_of(k)), device_id_type=MESH)
        return c

    lax.fori_loop(1, n, greet, 0)

    pad[...] = jnp.zeros_like(pad)
    pad[0:capacity, 0:n] = requests[...]
    turned = pad[...].T
    span = 128 // capacity
    wanted[:, 0, :] = jnp.concatenate(
        [jnp.broadcast_to(turned[0:n, r:r + 1], (n, span)) for r in range(capacity)], axis=1)

    for kind, source in enumerate((down_rows, up_rows)):
        for c in range(per_row):
            table[kind, c * rows:(c + 1) * rows, :] = source[:, c * chunk:(c + 1) * chunk]

    pl.semaphore_wait(barrier, n - 1)

    def ask_copy(peer):
        return pltpu.make_async_remote_copy(
            src_ref=wanted.at[peer], dst_ref=asked.at[me], send_sem=ask_send.at[peer],
            recv_sem=ask_recv.at[me], device_id=where(peer), device_id_type=MESH)

    def ask_start(k, c):
        ask_copy(peer_of(k)).start()
        return c

    lax.fori_loop(1, n, ask_start, 0)
    pltpu.make_async_copy(wanted.at[me], asked.at[me], ask_recv.at[me]).start()

    lanes = 256
    pairs = places.shape[0]

    def weigh(i, c):
        at = pl.ds(pl.multiple_of(i * lanes, lanes), lanes)
        for s0 in range(0, slots, 64):
            place = iota((64, lanes), 0) + s0
            total = jnp.zeros((64, lanes), F32)
            for p in range(pairs):
                total += jnp.where(places[p:p + 1, at] == place, gates[p:p + 1, at], jnp.float32(0))
            weight[s0:s0 + 64, at] = total
        return c

    lax.fori_loop(0, n_tok // lanes, weigh, 0)

    def select(g):
        ask = asked[g * GROUP:(g + 1) * GROUP, 0, :].astype(F32)
        both = jnp.concatenate(
            [jnp.broadcast_to(ask[:, r * span:r * span + 1], (GROUP, 128)) for r in range(capacity)], axis=0)
        r = iota((big, capacity * GROUP), 0)
        c = iota((big, capacity * GROUP), 1)
        spread = ones_where(
            (lax.rem(c, GROUP) == lax.div(r, message))
            & (lax.div(c, GROUP) == lax.div(lax.rem(r, message), per_row)))
        value = dot(spread, both.astype(BF16)).astype(jnp.int32)
        lane = iota((big, 128), 1)
        piece = lax.rem(iota((big, 128), 0), per_row)
        parts = []
        for t in range(per_row * rows // 128):
            full = lane + t * 128
            hit = (lax.rem(full, rows) == value) & (lax.div(full, rows) == piece)
            parts.append(jnp.where(hit, jnp.float32(1), jnp.float32(0)))
        return jnp.concatenate(parts, axis=1)

    def span_of(peer):
        return pl.ds(pl.multiple_of(peer * message, message), message)

    def exchange(source, target, send, recv, kind):
        def remote(peer):
            return pltpu.make_async_remote_copy(
                src_ref=source.at[kind, span_of(peer), :], dst_ref=target.at[kind, span_of(me), :],
                send_sem=send.at[kind, peer], recv_sem=recv.at[kind, me],
                device_id=where(peer), device_id_type=MESH)

        def start(i, c):
            @pl.when(i != me)
            def _():
                remote(i).start()

            @pl.when(i == me)
            def _():
                pltpu.make_async_copy(
                    source.at[kind, span_of(me), :], target.at[kind, span_of(me), :],
                    recv.at[kind, me]).start()
            return c

        def start_all(k, c):
            remote(peer_of(k)).start()
            return c

        def arrive(i, c):
            at = target.at[kind, span_of(i), :]
            pltpu.make_async_copy(at, at, recv.at[kind, i]).wait()
            return c

        def sent(k, c):
            remote(peer_of(k)).wait_send()
            return c

        def begin():
            lax.fori_loop(1, n, start_all, 0)
            pltpu.make_async_copy(
                source.at[kind, span_of(me), :], target.at[kind, span_of(me), :],
                recv.at[kind, me]).start()

        return (
            lambda g: lax.fori_loop(g * GROUP, (g + 1) * GROUP, start, 0),
            begin,
            lambda g: lax.fori_loop(g * GROUP, (g + 1) * GROUP, arrive, 0),
            lambda: lax.fori_loop(1, n, sent, 0),
        )

    row_moves = [exchange(msg_out, msg_in, row_send, row_recv, kind) for kind in range(2)]
    ret_moves = [exchange(ret_out, ret_in, ret_send, ret_recv, kind) for kind in range(2)]

    def ask_wait(i, c):
        pltpu.make_async_copy(asked.at[i], asked.at[i], ask_recv.at[i]).wait()
        return c

    for g in range(groups):
        at = slice(g * big, (g + 1) * big)
        lax.fori_loop(g * GROUP, (g + 1) * GROUP, ask_wait, 0)
        sel[at, :] = select(g)
        msg_out[0, at, :] = dot(sel[at, :].astype(BF16), table[0]).astype(BF16)
        row_moves[0][0](g)
    for g in range(groups):
        at = slice(g * big, (g + 1) * big)
        msg_out[1, at, :] = dot(sel[at, :].astype(BF16), table[1]).astype(BF16)
        row_moves[1][0](g)
    for g in range(groups):
        at = slice(g * big, (g + 1) * big)
        sel_t[:, at] = sel[at, :].T.astype(BF16)

    seats = GROUP * capacity
    r = iota((big, big), 0)
    c = iota((big, big), 1)
    unpack = ones_where(
        (lax.div(r, seats) == lax.rem(c, per_row)) & (lax.rem(r, seats) == lax.div(c, per_row)))
    pack = ones_where(
        (lax.div(c, seats) == lax.rem(r, per_row)) & (lax.rem(c, seats) == lax.div(r, per_row)))

    def fetch(kind, target, base):
        for g in range(groups):
            row_moves[kind][2](g)
            laid = dot(unpack, msg_in[kind, g * big:(g + 1) * big, :]).astype(BF16)
            at = pl.ds(pl.multiple_of(base + g * seats, seats), seats)
            for j in range(per_row):
                target[at, j * chunk:(j + 1) * chunk] = laid[j * seats:(j + 1) * seats, :]

    def put_back(kind):
        for g in range(groups):
            pieces = [
                part[kind, g * seats:(g + 1) * seats, j * chunk:(j + 1) * chunk].astype(BF16)
                for j in range(per_row)
            ]
            ret_out[kind, g * big:(g + 1) * big, :] = dot(
                pack, jnp.concatenate(pieces, axis=0)).astype(BF16)
        ret_moves[kind][1]()

    def slots_of(q):
        return pl.ds(pl.multiple_of(q * slots, slots), slots)

    own = slots_of(model_at)
    sibling = model_at + 1 - 2 * lax.rem(model_at, 2)

    def down_copy(q, to, sem):
        return pltpu.make_async_remote_copy(
            src_ref=f_down.at[slots_of(q), :], dst_ref=f_down.at[slots_of(q), :],
            send_sem=down_send.at[sem], recv_sem=down_recv.at[q],
            device_id=(data_at, to), device_id_type=MESH)

    def same_core(j):
        return lax.rem(model_at + 2 * j, n_model)

    def down_wait(q):
        at = f_down.at[slots_of(q), :]
        pltpu.make_async_copy(at, at, down_recv.at[q]).wait()

    fetch(0, f_down, model_at * slots)
    for j in range(1, lines):
        down_copy(model_at, same_core(j), j).start()
    down_copy(model_at, sibling, 0).start()

    for b in range(n_model):
        at = slice(b * block, (b + 1) * block)
        tok_copy(b).wait()
        pre = dot(f_down[own, :], tok[at, :], ((1,), (1,)))
        active, slope = gelu_parts(pre)
        w = weight[:, at]
        gated[:, at] = (w * active).astype(BF16)
        weight[:, at] = w * slope
    for b in range(n_model):
        grd_copy(b).wait()
    step = 512
    for c0 in range(0, width, step):
        part[1, :, c0:c0 + step] = dot(gated[...], grd[:, c0:c0 + step])
    put_back(1)

    for j in range(1, lines):
        down_wait(same_core(j))
        down_copy(same_core(j), sibling, lines + j).start()

    fetch(1, f_up, 0)
    for b in range(n_model):
        at = slice(b * block, (b + 1) * block)
        back = dot(f_up[...], grd[at, :], ((1,), (1,)))
        coef = (weight[:, at] * back).astype(BF16)
        coef_out[b] = coef
        gated[:, at] = coef

    def coef_copy(j, k):
        return pltpu.make_async_remote_copy(
            src_ref=coef_out.at[j], dst_ref=coef_in.at[own, :],
            send_sem=coef_send.at[k], recv_sem=coef_recv.at[k],
            device_id=(data_at, j), device_id_type=MESH)

    for k in range(1, n_model):
        coef_copy(lax.rem(model_at + k, n_model), k).start()
    own_coef = pltpu.make_async_copy(coef_out.at[model_at], coef_in.at[own, :], coef_recv.at[0])
    own_coef.start()

    for c0 in range(0, width, step):
        part[0, :, c0:c0 + step] = dot(gated[...], tok[:, c0:c0 + step])
    put_back(0)

    down_wait(sibling)
    for j in range(1, lines):
        down_wait(lax.rem(sibling + 2 * j, n_model))
    own_coef.wait()
    for k in range(1, n_model):
        there = coef_in.at[slots_of(lax.rem(model_at + n_model - k, n_model)), :]
        pltpu.make_async_copy(there, there, coef_recv.at[k]).wait()
    coef_t[...] = coef_in[...].astype(F32).T.astype(BF16)

    def finish(i, c):
        at = pl.ds(pl.multiple_of(i * step, step), step)
        input_grad[:, at] = dot(coef_t[...], f_down[:, at]).astype(BF16)
        return c

    lax.fori_loop(0, width // step, finish, 0)

    for kind, target in ((1, up_grad), (0, down_grad)):
        for g in range(groups):
            ret_moves[kind][2](g)
        for c0 in range(per_row):
            target[:, c0 * chunk:(c0 + 1) * chunk] = dot(
                sel_t[c0 * rows:(c0 + 1) * rows, :], ret_in[kind])

    def ask_sent(k, c):
        ask_copy(peer_of(k)).wait_send()
        return c

    lax.fori_loop(1, n, ask_sent, 0)
    for kind in range(2):
        row_moves[kind][3]()
        ret_moves[kind][3]()
    down_copy(model_at, sibling, 0).wait_send()
    for j in range(1, lines):
        down_copy(model_at, same_core(j), j).wait_send()
        down_copy(same_core(j), sibling, lines + j).wait_send()
    for k in range(1, n_model):
        coef_copy(lax.rem(model_at + k, n_model), k).wait_send()


def shards(tokens, out_grad, down_rows, up_rows, requests, places, gate_weights):
    n_model = lax.axis_size("mp")
    n = lax.axis_size("dp") * n_model
    rows, width = down_rows.shape
    n_tok = tokens.shape[0]
    capacity = requests.shape[2]
    slots = n * capacity
    block = n_tok // n_model
    chunk = width // PIECES
    moved = n * capacity * PIECES
    wanted = jnp.transpose(requests[0], (1, 0))
    chosen = jnp.transpose(places, (0, 2, 1)).reshape(-1, n_tok)
    gates = jnp.transpose(gate_weights, (0, 2, 1)).reshape(-1, n_tok)
    vmem = pl.BlockSpec(memory_space=pltpu.VMEM)
    hbm = pl.BlockSpec(memory_space=pltpu.HBM)
    dma = pltpu.SemaphoreType.DMA
    flops = 10 * n_tok * slots * width
    buffers = [
        ((n_tok, width), BF16),
        ((n_tok, width), BF16),
        ((128, 128), jnp.int32),
        ((n, 1, 128), jnp.int32),
        ((n, 1, 128), jnp.int32),
        ((2, PIECES * rows, chunk), BF16),
        ((moved, PIECES * rows), F32),
        ((PIECES * rows, moved), BF16),
        ((2, moved, chunk), BF16),
        ((2, moved, chunk), BF16),
        ((2, moved, chunk), BF16),
        ((2, moved, chunk), BF16),
        ((n_model * slots, width), BF16),
        ((slots, width), BF16),
        ((slots, n_tok), F32),
        ((slots, n_tok), BF16),
        ((n_model, slots, block), BF16),
        ((n_model * slots, block), BF16),
        ((block, n_model * slots), BF16),
        ((2, slots, width), F32),
    ]
    taken = sum(math.prod(shape) * jnp.dtype(kind).itemsize for shape, kind in buffers)
    ends = block * width * 2 + rows * width * 12 + chosen.size * 8
    return pl.pallas_call(
        functools.partial(kernel, n, n_model),
        out_shape=(
            jax.ShapeDtypeStruct((block, width), BF16),
            jax.ShapeDtypeStruct((rows, width), F32),
            jax.ShapeDtypeStruct((rows, width), F32),
        ),
        in_specs=[hbm, hbm, vmem, vmem, vmem, vmem, vmem],
        out_specs=(vmem, vmem, vmem),
        scratch_shapes=[pltpu.VMEM(shape, kind) for shape, kind in buffers] + [
            dma((n_model,)), dma((n_model,)), dma((n,)), dma((n,)),
            dma((2, n)), dma((2, n)), dma((2, n)), dma((2, n)),
            dma((n_model,)), dma((n_model,)), dma((n_model,)), dma((n_model,)),
        ],
        compiler_params=pltpu.CompilerParams(
            collective_id=0, has_side_effects=True, vmem_limit_bytes=taken + ends + SPARE),
        cost_estimate=pl.CostEstimate(
            flops=flops, bytes_accessed=4 * n_tok * width, transcendentals=2 * n_tok * slots),
    )(tokens, out_grad, down_rows, up_rows, wanted, chosen, gates)


def solution(mesh):
    in_specs = (
        P("dp", None),
        P("dp", None),
        P(("dp", "mp"), None),
        P(("dp", "mp"), None),
        P(("dp", "mp"), None, None),
        P("mp", "dp", None),
        P("mp", "dp", None),
    )
    out_specs = (P(("dp", "mp"), None), P(("dp", "mp"), None), P(("dp", "mp"), None))
    return jax.shard_map(shards, mesh=mesh, in_specs=in_specs, out_specs=out_specs, check_vma=False)
```

```python
import functools
import math

import jax
import jax.numpy as jnp
from jax import lax
from jax.experimental import pallas as pl
from jax.experimental.pallas import tpu as pltpu
from jax.sharding import PartitionSpec as P

SQRT_HALF = 0.7071067811865476
INV_ROOT_TAU = 0.3989422804014327
F32 = jnp.float32
BF16 = jnp.bfloat16
GROUP = 8
PIECES = 8
SPARE = 4 * 1024 * 1024
GRANT = 46 * 1024 * 1024
MESH = pl.DeviceIdType.MESH


def gelu_parts(pre):
    normal_cdf = 0.5 * (1.0 + lax.erf(pre * SQRT_HALF))
    density = INV_ROOT_TAU * jnp.exp(-0.5 * pre * pre)
    return (pre * normal_cdf, normal_cdf + pre * density)


def iota(shape, dim):
    return lax.broadcasted_iota(jnp.int32, shape, dim)


def div(values, by):
    if by & (by - 1) == 0:
        return lax.shift_right_logical(values, jnp.full_like(values, by.bit_length() - 1))
    return lax.div(values, by)


def rem(values, by):
    if by & (by - 1) == 0:
        return values & (by - 1)
    return lax.rem(values, by)


def ones_where(mask):
    return jnp.where(mask, jnp.float32(1), jnp.float32(0)).astype(BF16)


def dot(a, b, dims=((1,), (0,))):
    return lax.dot_general(a, b, (dims, ((), ())), preferred_element_type=F32)


def kernel(
    n, n_model, tokens, grads, down_rows, up_rows, requests, places, gates,
    input_grad, down_grad, up_grad,
    tok, grd, pad, wanted, asked, table, sel, sel_t, msg_out, msg_in, ret_out, ret_in,
    f_down, f_up, weight, gated, coef_out, coef_in, coef_t, part,
    tok_sem, grd_sem, ask_send, ask_recv, row_send, row_recv, ret_send, ret_recv,
    down_send, down_recv, coef_send, coef_recv,
):
    data_at = lax.axis_index("dp")
    model_at = lax.axis_index("mp")
    me = data_at * n_model + model_at
    rows, width = down_rows.shape
    capacity = requests.shape[0]
    per_row = PIECES
    chunk = width // per_row
    message = capacity * per_row
    slots = n * capacity
    n_tok = tok.shape[0]
    block = n_tok // n_model
    big = GROUP * message
    groups = n // GROUP
    lines = n_model // 2

    def tok_copy(j):
        at = pl.ds(j * block, block)
        return pltpu.make_async_copy(tokens.at[at, :], tok.at[at, :], tok_sem.at[j])

    def grd_copy(j):
        at = pl.ds(j * block, block)
        return pltpu.make_async_copy(grads.at[at, :], grd.at[at, :], grd_sem.at[j])

    for j in range(n_model):
        tok_copy(j).start()
    for j in range(n_model):
        grd_copy(j).start()

    n_data = n // n_model

    def others(act):
        def line(k, c):
            p = data_at + k
            p = jnp.where(p >= n_data, p - n_data, p)
            for q in range(n_model):
                peer = p * n_model + q

                @pl.when(peer != me)
                def _():
                    act(peer, (p, q))
            return c

        lax.fori_loop(0, n_data, line, 0)

    barrier = pltpu.get_barrier_semaphore()
    others(lambda peer, to: pl.semaphore_signal(
        barrier, inc=1, device_id=to, device_id_type=MESH))

    pad[...] = jnp.zeros_like(pad)
    pad[0:capacity, 0:n] = requests[...]
    turned = pad[...].T
    span = 128 // capacity
    wanted[:, 0, :] = jnp.concatenate(
        [jnp.broadcast_to(turned[0:n, r:r + 1], (n, span)) for r in range(capacity)], axis=1)

    for kind, source in enumerate((down_rows, up_rows)):
        for c in range(per_row):
            table[kind, c * rows:(c + 1) * rows, :] = source[:, c * chunk:(c + 1) * chunk]

    pl.semaphore_wait(barrier, n - 1)

    def ask_copy(peer, to):
        return pltpu.make_async_remote_copy(
            src_ref=wanted.at[peer], dst_ref=asked.at[me], send_sem=ask_send.at[peer],
            recv_sem=ask_recv.at[me], device_id=to, device_id_type=MESH)

    others(lambda peer, to: ask_copy(peer, to).start())
    pltpu.make_async_copy(wanted.at[me], asked.at[me], ask_recv.at[me]).start()

    lanes = 256
    pairs = places.shape[0]

    def weigh(i, c):
        at = pl.ds(pl.multiple_of(i * lanes, lanes), lanes)
        for s0 in range(0, slots, 64):
            place = iota((64, lanes), 0) + s0
            total = jnp.zeros((64, lanes), F32)
            for p in range(pairs):
                total += jnp.where(places[p:p + 1, at] == place, gates[p:p + 1, at], jnp.float32(0))
            weight[s0:s0 + 64, at] = total
        return c

    lax.fori_loop(0, n_tok // lanes, weigh, 0)

    def select(g):
        ask = asked[g * GROUP:(g + 1) * GROUP, 0, :].astype(F32)
        both = jnp.concatenate(
            [jnp.broadcast_to(ask[:, r * span:r * span + 1], (GROUP, 128)) for r in range(capacity)], axis=0)
        r = iota((big, capacity * GROUP), 0)
        c = iota((big, capacity * GROUP), 1)
        spread = ones_where(
            (rem(c, GROUP) == div(r, message))
            & (div(c, GROUP) == div(rem(r, message), per_row)))
        value = dot(spread, both.astype(BF16)).astype(jnp.int32)
        lane = iota((big, 128), 1)
        piece = rem(iota((big, 128), 0), per_row)
        parts = []
        for t in range(per_row * rows // 128):
            full = lane + t * 128
            hit = (rem(full, rows) == value) & (div(full, rows) == piece)
            parts.append(jnp.where(hit, jnp.float32(1), jnp.float32(0)))
        return jnp.concatenate(parts, axis=1)

    def span_of(peer):
        return pl.ds(pl.multiple_of(peer * message, message), message)

    def exchange(source, target, send, recv, kind):
        def remote(peer, to):
            return pltpu.make_async_remote_copy(
                src_ref=source.at[kind, span_of(peer), :], dst_ref=target.at[kind, span_of(me), :],
                send_sem=send.at[kind, peer], recv_sem=recv.at[kind, me],
                device_id=to, device_id_type=MESH)

        def keep():
            pltpu.make_async_copy(
                source.at[kind, span_of(me), :], target.at[kind, span_of(me), :],
                recv.at[kind, me]).start()

        def start(g):
            for i in range(g * GROUP, (g + 1) * GROUP):
                @pl.when(i != me)
                def _():
                    remote(i, (i // n_model, i % n_model)).start()

                @pl.when(i == me)
                def _():
                    keep()

        def arrive(i, c):
            at = target.at[kind, span_of(i), :]
            pltpu.make_async_copy(at, at, recv.at[kind, i]).wait()
            return c

        def begin():
            others(lambda peer, to: remote(peer, to).start())
            keep()

        return (
            start,
            begin,
            lambda g: lax.fori_loop(g * GROUP, (g + 1) * GROUP, arrive, 0),
            lambda: others(lambda peer, to: remote(peer, to).wait_send()),
        )

    row_moves = [exchange(msg_out, msg_in, row_send, row_recv, kind) for kind in range(2)]
    ret_moves = [exchange(ret_out, ret_in, ret_send, ret_recv, kind) for kind in range(2)]

    def ask_wait(i, c):
        pltpu.make_async_copy(asked.at[i], asked.at[i], ask_recv.at[i]).wait()
        return c

    for g in range(groups):
        at = slice(g * big, (g + 1) * big)
        lax.fori_loop(g * GROUP, (g + 1) * GROUP, ask_wait, 0)
        sel[at, :] = select(g)
        msg_out[0, at, :] = dot(sel[at, :].astype(BF16), table[0]).astype(BF16)
        row_moves[0][0](g)
    for g in range(groups):
        at = slice(g * big, (g + 1) * big)
        msg_out[1, at, :] = dot(sel[at, :].astype(BF16), table[1]).astype(BF16)
        row_moves[1][0](g)
    for g in range(groups):
        at = slice(g * big, (g + 1) * big)
        sel_t[:, at] = sel[at, :].T.astype(BF16)

    seats = GROUP * capacity
    r = iota((big, big), 0)
    c = iota((big, big), 1)
    unpack = ones_where(
        (div(r, seats) == rem(c, per_row)) & (rem(r, seats) == div(c, per_row)))
    pack = ones_where(
        (div(c, seats) == rem(r, per_row)) & (rem(c, seats) == div(r, per_row)))

    def fetch(kind, target, base):
        for g in range(groups):
            row_moves[kind][2](g)
            laid = dot(unpack, msg_in[kind, g * big:(g + 1) * big, :]).astype(BF16)
            at = pl.ds(pl.multiple_of(base + g * seats, seats), seats)
            for j in range(per_row):
                target[at, j * chunk:(j + 1) * chunk] = laid[j * seats:(j + 1) * seats, :]

    def put_back(kind):
        for g in range(groups):
            pieces = [
                part[kind, g * seats:(g + 1) * seats, j * chunk:(j + 1) * chunk].astype(BF16)
                for j in range(per_row)
            ]
            ret_out[kind, g * big:(g + 1) * big, :] = dot(
                pack, jnp.concatenate(pieces, axis=0)).astype(BF16)
        ret_moves[kind][1]()

    def slots_of(q):
        return pl.ds(pl.multiple_of(q * slots, slots), slots)

    own = slots_of(model_at)
    sibling = model_at + 1 - 2 * lax.rem(model_at, 2)

    def down_copy(q, to, sem):
        return pltpu.make_async_remote_copy(
            src_ref=f_down.at[slots_of(q), :], dst_ref=f_down.at[slots_of(q), :],
            send_sem=down_send.at[sem], recv_sem=down_recv.at[q],
            device_id=(data_at, to), device_id_type=MESH)

    def same_core(j):
        return lax.rem(model_at + 2 * j, n_model)

    def down_wait(q):
        at = f_down.at[slots_of(q), :]
        pltpu.make_async_copy(at, at, down_recv.at[q]).wait()

    fetch(0, f_down, model_at * slots)
    for j in range(1, lines):
        down_copy(model_at, same_core(j), j).start()
    down_copy(model_at, sibling, 0).start()

    for b in range(n_model):
        at = slice(b * block, (b + 1) * block)
        tok_copy(b).wait()
        pre = dot(f_down[own, :], tok[at, :], ((1,), (1,)))
        active, slope = gelu_parts(pre)
        w = weight[:, at]
        gated[:, at] = (w * active).astype(BF16)
        weight[:, at] = w * slope
    for b in range(n_model):
        grd_copy(b).wait()
    step = 512
    for c0 in range(0, width, step):
        part[1, :, c0:c0 + step] = dot(gated[...], grd[:, c0:c0 + step])
    put_back(1)

    for j in range(1, lines):
        down_wait(same_core(j))
        down_copy(same_core(j), sibling, lines + j).start()

    fetch(1, f_up, 0)
    for b in range(n_model):
        at = slice(b * block, (b + 1) * block)
        back = dot(f_up[...], grd[at, :], ((1,), (1,)))
        coef = (weight[:, at] * back).astype(BF16)
        coef_out[b] = coef
        gated[:, at] = coef

    def coef_copy(j, k):
        return pltpu.make_async_remote_copy(
            src_ref=coef_out.at[j], dst_ref=coef_in.at[own, :],
            send_sem=coef_send.at[k], recv_sem=coef_recv.at[k],
            device_id=(data_at, j), device_id_type=MESH)

    for k in range(1, n_model):
        coef_copy(lax.rem(model_at + k, n_model), k).start()
    own_coef = pltpu.make_async_copy(coef_out.at[model_at], coef_in.at[own, :], coef_recv.at[0])
    own_coef.start()

    for c0 in range(0, width, step):
        part[0, :, c0:c0 + step] = dot(gated[...], tok[:, c0:c0 + step])
    put_back(0)

    down_wait(sibling)
    for j in range(1, lines):
        down_wait(lax.rem(sibling + 2 * j, n_model))
    own_coef.wait()
    for k in range(1, n_model):
        there = coef_in.at[slots_of(lax.rem(model_at + n_model - k, n_model)), :]
        pltpu.make_async_copy(there, there, coef_recv.at[k]).wait()
    coef_t[...] = coef_in[...].astype(F32).T.astype(BF16)

    def finish(i, c):
        at = pl.ds(pl.multiple_of(i * step, step), step)
        input_grad[:, at] = dot(coef_t[...], f_down[:, at]).astype(BF16)
        return c

    lax.fori_loop(0, width // step, finish, 0)

    for kind, target in ((1, up_grad), (0, down_grad)):
        for g in range(groups):
            ret_moves[kind][2](g)
        for c0 in range(per_row):
            target[:, c0 * chunk:(c0 + 1) * chunk] = dot(
                sel_t[c0 * rows:(c0 + 1) * rows, :], ret_in[kind])

    others(lambda peer, to: ask_copy(peer, to).wait_send())
    for kind in range(2):
        row_moves[kind][3]()
        ret_moves[kind][3]()
    down_copy(model_at, sibling, 0).wait_send()
    for j in range(1, lines):
        down_copy(model_at, same_core(j), j).wait_send()
        down_copy(same_core(j), sibling, lines + j).wait_send()
    for k in range(1, n_model):
        coef_copy(lax.rem(model_at + k, n_model), k).wait_send()


def shards(tokens, out_grad, down_rows, up_rows, requests, places, gate_weights):
    n_model = lax.axis_size("mp")
    n = lax.axis_size("dp") * n_model
    rows, width = down_rows.shape
    n_tok = tokens.shape[0]
    capacity = requests.shape[2]
    slots = n * capacity
    block = n_tok // n_model
    chunk = width // PIECES
    moved = n * capacity * PIECES
    wanted = jnp.transpose(requests[0], (1, 0))
    chosen = jnp.transpose(places, (0, 2, 1)).reshape(-1, n_tok)
    gates = jnp.transpose(gate_weights, (0, 2, 1)).reshape(-1, n_tok)
    vmem = pl.BlockSpec(memory_space=pltpu.VMEM)
    hbm = pl.BlockSpec(memory_space=pltpu.HBM)
    dma = pltpu.SemaphoreType.DMA
    flops = 10 * n_tok * slots * width
    buffers = [
        ((n_tok, width), BF16),
        ((n_tok, width), BF16),
        ((128, 128), jnp.int32),
        ((n, 1, 128), jnp.int32),
        ((n, 1, 128), jnp.int32),
        ((2, PIECES * rows, chunk), BF16),
        ((moved, PIECES * rows), F32),
        ((PIECES * rows, moved), BF16),
        ((2, moved, chunk), BF16),
        ((2, moved, chunk), BF16),
        ((2, moved, chunk), BF16),
        ((2, moved, chunk), BF16),
        ((n_model * slots, width), BF16),
        ((slots, width), BF16),
        ((slots, n_tok), F32),
        ((slots, n_tok), BF16),
        ((n_model, slots, block), BF16),
        ((n_model * slots, block), BF16),
        ((block, n_model * slots), BF16),
        ((2, slots, width), F32),
    ]
    taken = sum(math.prod(shape) * jnp.dtype(kind).itemsize for shape, kind in buffers)
    ends = block * width * 2 + rows * width * 12 + chosen.size * 8
    return pl.pallas_call(
        functools.partial(kernel, n, n_model),
        out_shape=(
            jax.ShapeDtypeStruct((block, width), BF16),
            jax.ShapeDtypeStruct((rows, width), F32),
            jax.ShapeDtypeStruct((rows, width), F32),
        ),
        in_specs=[hbm, hbm, vmem, vmem, vmem, vmem, vmem],
        out_specs=(vmem, vmem, vmem),
        scratch_shapes=[pltpu.VMEM(shape, kind) for shape, kind in buffers] + [
            dma((n_model,)), dma((n_model,)), dma((n,)), dma((n,)),
            dma((2, n)), dma((2, n)), dma((2, n)), dma((2, n)),
            dma((n_model,)), dma((n_model,)), dma((n_model,)), dma((n_model,)),
        ],
        compiler_params=pltpu.CompilerParams(
            collective_id=0, has_side_effects=True, vmem_limit_bytes=max(taken + ends + SPARE, GRANT)),
        cost_estimate=pl.CostEstimate(
            flops=flops, bytes_accessed=4 * n_tok * width, transcendentals=2 * n_tok * slots),
    )(tokens, out_grad, down_rows, up_rows, wanted, chosen, gates)


def solution(mesh):
    in_specs = (
        P("dp", None),
        P("dp", None),
        P(("dp", "mp"), None),
        P(("dp", "mp"), None),
        P(("dp", "mp"), None, None),
        P("mp", "dp", None),
        P("mp", "dp", None),
    )
    out_specs = (P(("dp", "mp"), None), P(("dp", "mp"), None), P(("dp", "mp"), None))
    return jax.shard_map(shards, mesh=mesh, in_specs=in_specs, out_specs=out_specs, check_vma=False)
```
